128 devices in a mesh: centers: 32 (over y, z_hi, x), nys: 4 (over z_lo, core).
Axes of the slice: x: 4, y: 4, z: 4 (z_hi: 2, z_lo: 2; z = z_hi * 2 + z_lo), core: 2. Of those that a mesh axis runs over, the one named last changes fastest.
Arguments:
- centers: bfloat16 [262144, 1024], P(('centers', 'nys'))
- weights: bfloat16 [262144, 1000], P(('centers', 'nys')), may hold values from -1.5 to 1.5
- labels: bfloat16 [262144, 1000], P(('centers', 'nys')), may hold values from -6 to 6
- loader: int32 [1], replicated, may hold values from 0 to 127
- sample_ids: int32 [1024], replicated, may hold values from 0 to 2047, as said below
- nys_ids: int32 [16384], P(('centers', 'nys')), may hold values from 0 to 2047, as said below
- eigen_vectors: bfloat16 [16384, 160], P('centers', 'nys'), may hold values from -0.046875 to 0.046875
- eigen_scale: float32 [160], replicated, may hold values from 2 to 40
Outputs:
- new_weights: bfloat16 [262144, 1000], P(('centers', 'nys'))
- residual: bfloat16 [1024, 1000], replicated
The draws below stay inside these ranges and needn't reach their ends.
Inputs may be any that keep to these rules, and one draw needn't show every extreme that they name: `sample_ids`: each entry is a row of the loader's block of 2048 centers; repeats may occur. `nys_ids`: entry j is a row of the block of 2048 centers with the same block index as row j of the subsample; repeats may occur.
All inputs are finite; a program needn't handle non-finite values.
Results may differ from the reference program's by a relative error of at most 0.0095.
Values may be sent and summed in bfloat16 or wider, within the bound.
A program may use at most 128 MiB of HBM per device.

```python
import math
import jax
import jax.numpy as jnp
from jax import lax

D = 1024
OUT = 1000
Q = 160
BATCH = 1024
C_DEV = 2048
NYS_DEV = 128
SHARDS = 128
CENTERS = 262144
SUBSAMPLE = 16384


copies_per_image = 8


jitter_size = 0.1


def spread_ids(key, row_count, upper_id):
    subkeys = jax.random.split(key, 3)
    row_ids = jax.random.randint(subkeys[0], (row_count,), 0, upper_id)
    first_pos = jax.random.randint(subkeys[1], (), 0, row_count)
    second_pos = (first_pos + 1 + jax.random.randint(subkeys[2], (), 0, row_count - 1)) % row_count
    places = jnp.arange(row_count, dtype=jnp.int32)
    row_ids = jnp.where(places == first_pos, upper_id - 1, row_ids)
    row_ids = jnp.where(places == second_pos, 0, row_ids)
    return row_ids.astype(jnp.int32)


def draw_centers(key, part):
    key = jax.random.fold_in(key, 11)
    subkeys = jax.random.split(key, 5)
    group_count = max(CENTERS // copies_per_image, 1)
    order = jax.random.permutation(subkeys[0], CENTERS)
    group_of = (order % group_count).astype(jnp.int32)
    ranks = jax.random.permutation(subkeys[1], D).astype(jnp.float32)
    spread = 1.0 / jnp.sqrt((ranks + 1.0) * (math.log(D) + 0.5772))
    log_scale = jax.random.uniform(subkeys[2], (group_count, 1), jnp.float32, math.log(0.5), math.log(2.0))
    base_part = jax.random.normal(subkeys[3], (group_count, D), jnp.float32)
    jitter_part = jax.random.normal(subkeys[4], (CENTERS, D), jnp.float32)
    group_scale = jnp.exp(log_scale)
    group_rows = group_scale * base_part * spread[None, :]
    point_scale = jnp.take(group_scale, group_of, axis=0)
    points = jnp.take(group_rows, group_of, axis=0) + point_scale * (jitter_size / math.sqrt(D)) * jitter_part
    return points.astype(jnp.bfloat16)


def draw_sample_ids(key, part):
    key = jax.random.fold_in(key, 23)
    return spread_ids(key, BATCH, C_DEV)


def draw_nys_ids(key, part):
    key = jax.random.fold_in(key, 37)
    return spread_ids(key, SUBSAMPLE, C_DEV)


def steps_of(rng, dims, shards, low, largest):
    factor_of = 1.0
    for position, shards_of in shards:
        heights = jax.random.uniform(jax.random.fold_in(jax.random.fold_in(rng, 6), position), (shards_of,), jnp.float32, low / len(shards), largest / len(shards))
        factor_of = factor_of * jnp.repeat(jnp.exp(heights), dims[position] // shards_of).reshape((-1,) + (1,) * (len(dims) - 1 - position))
    return factor_of


def noise(stream_key, dims, width, reach, pieces=(), kind=jnp.bfloat16):
    drawn = jax.random.normal(stream_key, dims, jnp.float32) * width
    if len(pieces) > 0:
        drawn = steps_of(stream_key, dims, pieces, -0.22, 0.18) * drawn
    return jnp.clip(drawn, min=-reach, max=reach).astype(kind)


def setup_inputs(seed: int = 0) -> dict:
    streams_of = jax.random.split(jax.random.key(seed), 9)
    centers = draw_centers(jax.random.fold_in(streams_of[8], 71), 0)
    weights = noise(streams_of[1], (CENTERS, OUT), 0.25, 1.5, ((0, 128),))
    labels = noise(streams_of[2], (CENTERS, OUT), 1.0, 6.0, ((0, 128),))
    loader = jax.random.randint(streams_of[3], (1,), 0, SHARDS).astype(jnp.int32)
    sample_ids = draw_sample_ids(jax.random.fold_in(streams_of[8], 71), 0)
    nys_ids = draw_nys_ids(jax.random.fold_in(streams_of[8], 71), 0)
    eigen_vectors = noise(streams_of[6], (SUBSAMPLE, Q), SUBSAMPLE ** -0.5, 0.046875, ((0, 32), (1, 4)))
    eigen_scale = jnp.clip(jnp.exp(jax.random.uniform(streams_of[7], (Q,), jnp.float32, math.log(2.0), math.log(40.0))), 2.0, 40.0)
    return {"centers": centers, "weights": weights, "labels": labels, "loader": loader, "sample_ids": sample_ids, "nys_ids": nys_ids, "eigen_vectors": eigen_vectors, "eigen_scale": eigen_scale}


learn_rate = 0.5
kernel_width = 0.25

def kernel(left_rows, right_rows):
    left_sq = lax.optimization_barrier(jnp.sum(jnp.square(left_rows.astype(jnp.float32)), axis=1))
    right_sq = lax.optimization_barrier(jnp.sum(jnp.square(right_rows.astype(jnp.float32)), axis=1))
    inner_prod = lax.dot_general(left_rows, right_rows, (((1,), (1,)), ((), ())), preferred_element_type=jnp.float32)
    distance = jnp.sqrt(jnp.maximum(left_sq[:, None] + right_sq[None, :] - 2.0 * inner_prod, 0.0))
    return jnp.exp(-distance / kernel_width).astype(jnp.bfloat16)

def reference(centers, weights, labels, loader, sample_ids, nys_ids, eigen_vectors, eigen_scale):
    batch_rows = (loader[0] * C_DEV + sample_ids).astype(jnp.int32)
    minibatch = jnp.take(centers, batch_rows, axis=0)
    targets = jnp.take(labels, batch_rows, axis=0)
    center_blocks = centers.reshape(SHARDS, C_DEV, D)
    weight_blocks = weights.reshape(SHARDS, C_DEV, OUT)

    def add_block(summed_rows, block_pair):
        kernel_rows = kernel(minibatch, block_pair[0])
        return (summed_rows + jnp.dot(kernel_rows, block_pair[1], preferred_element_type=jnp.float32), None)
    summed_rows, _ = lax.scan(add_block, jnp.zeros((BATCH, OUT), jnp.float32), (center_blocks, weight_blocks))
    residual = (summed_rows - targets.astype(jnp.float32)).astype(jnp.bfloat16)
    owners = jnp.arange(SUBSAMPLE, dtype=jnp.int32) // NYS_DEV
    sub_rows = (owners * C_DEV + nys_ids).astype(jnp.int32)
    subsample = jnp.take(centers, sub_rows, axis=0)
    kernel_sub = kernel(subsample, minibatch)
    projected = jnp.dot(kernel_sub, residual, preferred_element_type=jnp.float32).astype(jnp.bfloat16)
    reduced = lax.dot_general(eigen_vectors, projected, (((0,), (0,)), ((), ())), preferred_element_type=jnp.float32)
    coefficients = (eigen_scale[:, None] * reduced).astype(jnp.bfloat16)
    correction = jnp.dot(eigen_vectors, coefficients, preferred_element_type=jnp.float32)
    weight_step = jnp.zeros((CENTERS, OUT), jnp.float32).at[sub_rows].add(learn_rate * correction)
    weight_step = weight_step.at[batch_rows].add(-learn_rate * residual.astype(jnp.float32))
    new_weights = (weights.astype(jnp.float32) + weight_step).astype(jnp.bfloat16)
    return (new_weights, residual)
```

```python
import jax
import jax.numpy as jnp
from jax import lax
from jax.experimental import pallas as pl
from jax.experimental.pallas import tpu as pltpu
from jax.sharding import PartitionSpec as P

MESH = pl.DeviceIdType.MESH
BF16, F32 = jnp.bfloat16, jnp.float32

learn_rate = 0.5
kernel_width = 0.25

D, OUT, Q, BATCH, C_DEV, NYS_DEV = 1024, 1000, 160, 1024, 2048, 128
HALF = BATCH // 2
ROWS = 1280
EIG_ROW = 1008
BCAST_PARTS = (((0, 16), (0, 1, 2)), ((16, 16), (1, 2, 0)))
SUM_PARTS = (((0, 32), (0, 1, 2)), ((32, 32), (1, 2, 0)), ((64, 16), (2, 0, 1)))
NT = (((1,), (1,)), ((), ()))


def position():
    c, n = lax.axis_index("centers"), lax.axis_index("nys")
    x, y = lax.rem(c, 4), lax.div(c, 8)
    z = lax.rem(lax.div(c, 4), 2) * 2 + lax.div(n, 2)
    return (x, y, z), lax.rem(n, 2)


def device(chip, core):
    x, y, z = chip
    return ((y * 2 + lax.div(z, 2)) * 4 + x, lax.rem(z, 2) * 2 + core)


def peer_at(chip, core, axis, step):
    moved = list(chip)
    moved[axis] = lax.rem(chip[axis] + step, 4)
    return tuple(moved), device(moved, core)


def span(fixed, axis):
    return pl.ds(fixed[axis], 1) if axis in fixed else pl.ds(0, 4)


def bcast_index(core, part, fixed):
    (first, count), _ = part
    columns = pl.ds(pl.multiple_of(fixed[2] * 256, 256), 256) if 2 in fixed else pl.ds(0, D)
    return (pl.ds(core, 1), span(fixed, 0), span(fixed, 1), pl.ds(first, count), columns)


def sum_index(core, part, fixed):
    (first, count), _ = part
    if 2 in fixed:
        columns = pl.ds(pl.multiple_of(core * HALF + fixed[2] * 128, 128), 128)
    else:
        columns = pl.ds(pl.multiple_of(core * HALF, HALF), HALF)
    return (span(fixed, 0), span(fixed, 1), pl.ds(first, count), columns)


def bcast_shape(part, axes):
    (_, count), _ = part
    return (1, 1 if 0 in axes else 4, 1 if 1 in axes else 4, count, 256 if 2 in axes else D)


def sum_shape(part, axes):
    (_, count), _ = part
    return (1 if 0 in axes else 4, 1 if 1 in axes else 4, count, 128 if 2 in axes else HALF)


class Links:
    def __init__(self, send_sems, recv_sems):
        self.send_sems, self.recv_sems, self.copies = send_sems, recv_sems, []

    def start(self, source, target, to):
        i = len(self.copies)
        copy = pltpu.make_async_remote_copy(
            src_ref=source, dst_ref=target, send_sem=self.send_sems.at[i], recv_sem=self.recv_sems.at[i],
            device_id=to, device_id_type=MESH,
        )
        copy.start()
        self.copies.append(copy)
        return copy

    def wait_sends(self):
        for copy in self.copies:
            copy.wait_send()


def scatter_start(links, buffer, slots, index, chip, core, part, stage):
    axes = part[1]
    fixed = {a: chip[a] for a in axes[:stage]}
    out = []
    for step in (2, 1, 3):
        moved, to = peer_at(chip, core, axes[stage], step)
        share = {**fixed, axes[stage]: moved[axes[stage]]}
        out.append(links.start(buffer.at[index(core, part, share)], slots.at[step - 1], to))
    return out


def scatter_finish(copies, buffer, slots, index, chip, core, part, stage, result):
    for copy in copies:
        copy.wait_recv()
    own = index(core, part, {a: chip[a] for a in part[1][: stage + 1]})
    total = buffer[own].astype(F32)
    for step in range(3):
        total += slots[step].astype(F32)
    result[own] = total.astype(BF16)


def gather_start(links, buffer, index, chip, core, part, stage):
    axes = part[1]
    own = index(core, part, {a: chip[a] for a in axes[: stage + 1]})
    return [
        links.start(buffer.at[own], buffer.at[own], peer_at(chip, core, axes[stage], step)[1]) for step in (2, 1, 3)
    ]


def step_kernel(
    loader_ref, ids_ref, nys_ref, eig_ref, centers_hbm, weights_hbm, labels_hbm,
    sums_hbm, pick_hbm, spread_hbm,
    cent, wts, labs, pick, stack, kern, cand, mini, rows2d, cnorm, ncol, mnorm, total, summed,
    own_eig, got_eig, idcol, half_c, half_s, *rest,
):
    bslots = [rest[2 * s : 2 * s + 2] for s in range(3)]
    sslots = [rest[6 + 3 * s : 9 + 3 * s] for s in range(3)]
    send_sems, recv_sems, local_sems = rest[15:]
    chip, core = position()
    other = 1 - core
    links = Links(send_sems, recv_sems)
    sibling = device(chip, other)
    my_nys = lax.axis_index("nys")
    near = chip[0], chip[1], chip[2] + 1 - 2 * lax.rem(chip[2], 2)
    partners = [sibling, device(near, other)]
    for axis in range(3):
        partners += [peer_at(chip, core, axis, step)[1] for step in (1, 2, 3)]

    barrier = pltpu.get_barrier_semaphore()
    for to in partners:
        pl.semaphore_signal(barrier, inc=1, device_id=to, device_id_type=MESH)
    loads = [
        pltpu.make_async_copy(a, b, local_sems.at[i])
        for i, (a, b) in enumerate(((centers_hbm, cent), (weights_hbm, wts), (labels_hbm, labs)))
    ]
    for load in loads:
        load.start()

    away = loader_ref[0] - (lax.axis_index("centers") * 4 + my_nys)
    ids = jnp.minimum(ids_ref[...] + away * away * 4096, 4096).astype(F32)
    idcol[...] = jnp.broadcast_to(ids, (128, BATCH)).T
    own_eig[...] = eig_ref[...].astype(F32)

    def pick_block(block):
        rows = pl.ds(pl.multiple_of(block * 256, 256), 256)
        column_ids = idcol[rows, :].astype(jnp.int32)

        def put(k, _):
            lane = lax.broadcasted_iota(jnp.int32, (256, 128), 1) + k * 128
            pick[rows, pl.ds(pl.multiple_of(k * 128, 128), 128)] = jnp.where(lane == column_ids, 1.0, 0.0).astype(BF16)
            return 0

        lax.fori_loop(0, 16, put, 0, unroll=4)

    def candidate_block(half, s):
        block = half * 2 + s
        pick_block(block)
        rows = pl.ds(pl.multiple_of(block * 256, 256), 256)

        def put(k, _):
            columns = pl.ds(pl.multiple_of(k * 256, 256), 256)
            got = jnp.dot(pick[rows, :], cent[:, columns], preferred_element_type=F32)
            cand[pl.ds(half, 1), pl.ds(s * 2, 2), :, :, columns] = got.astype(BF16).reshape(1, 2, 4, 32, 256)
            return 0

        lax.fori_loop(0, 4, put, 0)
        return 0

    pl.semaphore_wait(barrier, len(partners))
    eig_copies = []
    for to_core, to_chip in ((other, chip), (core, near), (other, near)):
        to = device(to_chip, to_core)
        eig_copies.append(
            links.start(own_eig.at[:, pl.ds(pl.multiple_of(to[1] * 128, 128), 128)], got_eig.at[my_nys], to)
        )
    got_eig[my_nys] = own_eig[:, pl.ds(pl.multiple_of(my_nys * 128, 128), 128)]

    loads[0].wait()
    lax.fori_loop(0, 2, lambda s, _: candidate_block(other, s), 0)
    first = links.start(cand.at[other], half_c, sibling)
    lax.fori_loop(0, 2, lambda s, _: candidate_block(core, s), 0)
    first.wait_recv()

    def add_half(k, _):
        x, y = lax.div(k, 4), lax.rem(k, 4)
        cand[core, x, y] = (cand[core, x, y].astype(F32) + half_c[x, y].astype(F32)).astype(BF16)
        return 0

    lax.fori_loop(0, 16, add_half, 0)
    pick_out = pltpu.make_async_copy(pick, pick_hbm, local_sems.at[3])
    pick_out.start()

    def targets(x):
        def put(k, _):
            columns = pl.ds(pl.multiple_of(k * 256, 256), 256)
            wanted = pick[columns, :]
            if x < 3:
                got = lax.dot_general(labs[pl.ds(x * 320, 320), :], wanted, NT, preferred_element_type=F32)
            else:
                got = lax.dot_general(labs[pl.ds(960, 40), :], wanted, NT, preferred_element_type=F32)
                got = jnp.concatenate([got, jnp.zeros((280, 256), F32)], axis=0)
            total[x, :, :, columns] = got.astype(BF16).reshape(4, 80, 256)
            return 0

        lax.fori_loop(0, 4, put, 0)

    def center_norms():
        def put(k, _):
            rows = pl.ds(pl.multiple_of(k * 64, 64), 64)
            cnorm[rows, :] = jnp.sum(jnp.square(cent[rows, :].astype(F32)), axis=1, keepdims=True)
            return 0

        lax.fori_loop(0, 32, put, 0)

    def stack_rows():
        loads[1].wait()

        def put(k, _):
            rows = pl.ds(pl.multiple_of(k * 64, 64), 64)
            stack[rows, :] = wts[rows, :]
            return 0

        lax.fori_loop(0, 15, put, 0)

    def stack_tail():
        for copy in eig_copies:
            copy.wait_recv()
        vectors = got_eig[...].reshape(Q, NYS_DEV).astype(BF16)
        row_ids = jnp.broadcast_to(nys_ref[...].astype(F32), (128, 128)).T.astype(jnp.int32)

        def put(k, _):
            columns = pl.ds(pl.multiple_of(k * 128, 128), 128)
            lane = lax.broadcasted_iota(jnp.int32, (128, 128), 1) + k * 128
            chosen = jnp.where(lane == row_ids, 1.0, 0.0).astype(BF16)
            spread = jnp.dot(vectors, chosen, preferred_element_type=F32)
            tail = jnp.concatenate(
                [wts[pl.ds(960, 40), columns].astype(F32), jnp.zeros((8, 128), F32), spread, jnp.zeros((112, 128), F32)],
                axis=0,
            )
            stack[pl.ds(960, 320), columns] = tail.astype(BF16)
            return 0

        lax.fori_loop(0, 16, put, 0)

    def nothing():
        pass

    def first_work():
        loads[2].wait()
        targets(0)
        targets(1)
        center_norms()

    def second_work():
        stack_rows()

    def third_work():
        stack_tail()

    flights = [scatter_start(links, cand, bslots[0][p], bcast_index, chip, core, part, 0) for p, part in enumerate(BCAST_PARTS)]
    for stage, work in enumerate((first_work, second_work, third_work)):
        work()
        following = []
        for p, part in enumerate(BCAST_PARTS):
            last = stage == 2
            scatter_finish(
                flights[p], cand, bslots[stage][p], bcast_index, chip, core, part, stage, mini if last else cand
            )
            if last:
                following.append(gather_start(links, mini, bcast_index, chip, core, part, 2))
            else:
                following.append(
                    scatter_start(links, cand, bslots[stage + 1][p], bcast_index, chip, core, part, stage + 1)
                )
        flights = following
    swaps = []
    for stage, work in ((2, lambda: targets(2)), (1, lambda: targets(3)), (0, nothing)):
        work()
        following = []
        for p, part in enumerate(BCAST_PARTS):
            for copy in flights[p]:
                copy.wait_recv()
            if stage > 0:
                following.append(gather_start(links, mini, bcast_index, chip, core, part, stage - 1))
            else:
                whole = mini.at[bcast_index(core, part, {})]
                swaps.append(links.start(whole, whole, sibling))
        flights = following

    def kernel_half(half):
        offset = pl.multiple_of(half * HALF, HALF)

        def rows_of(k, _):
            rows = pl.ds(pl.multiple_of(k * 32, 32), 32)
            block = mini[half, lax.div(k, 4), lax.rem(k, 4)]
            rows2d[rows, :] = block
            norm = jnp.sum(jnp.square(block.astype(F32)), axis=1, keepdims=True)
            ncol[rows, :] = jnp.broadcast_to(norm, (32, 128))
            return 0

        lax.fori_loop(0, 16, rows_of, 0)
        mnorm[...] = ncol[...].T[0:8, :]

        def put(k, _):
            rows = pl.ds(pl.multiple_of(k * 256, 256), 256)
            inner = lax.dot_general(cent[rows, :], rows2d[...], NT, preferred_element_type=F32)
            square = jnp.maximum(cnorm[rows, :] + mnorm[0:1, :] - 2.0 * inner, 0.0)
            kern[rows, pl.ds(offset, HALF)] = jnp.exp(jnp.sqrt(square) * (-1.0 / kernel_width)).astype(BF16)
            return 0

        lax.fori_loop(0, 8, put, 0)

    kernel_half(core)
    for copy in swaps:
        copy.wait_recv()
    kernel_half(other)

    def product(half, x):
        columns = pl.ds(pl.multiple_of(half * HALF, HALF), HALF)
        rows = pl.ds(pl.multiple_of(x * 320, 320), 320)
        got = jnp.dot(stack[rows, :], kern[:, columns], preferred_element_type=F32).reshape(1, 4, 80, HALF)
        return got - total[pl.ds(x, 1), :, :, columns].astype(F32), columns

    halves = []
    for step in (1, 2, 3, 0):
        x = lax.rem(chip[0] + step, 4)
        got, columns = product(other, x)
        total[pl.ds(x, 1), :, :, columns] = got.astype(BF16)
        halves.append(links.start(total.at[pl.ds(x, 1), :, :, columns], half_s.at[pl.ds(x, 1)], sibling))
    flights = [[], [], []]
    for i, step in enumerate((1, 2, 3, 0)):
        x = lax.rem(chip[0] + step, 4)
        got, columns = product(core, x)
        halves[i].wait_recv()
        got += half_s[pl.ds(x, 1)].astype(F32)
        total[pl.ds(x, 1), :, :, columns] = got.astype(BF16)
        if step:
            moved, to = peer_at(chip, core, 0, step)
            flights[0].append(
                links.start(total.at[sum_index(core, SUM_PARTS[0], {0: x})], sslots[0][0].at[step - 1], to)
            )
    for p in (1, 2):
        flights[p] = scatter_start(links, total, sslots[0][p], sum_index, chip, core, SUM_PARTS[p], 0)
    for stage in range(3):
        following = []
        for p, part in enumerate(SUM_PARTS):
            last = stage == 2
            scatter_finish(
                flights[p], total, sslots[stage][p], sum_index, chip, core, part, stage, summed if last else total
            )
            if last:
                following.append(gather_start(links, summed, sum_index, chip, core, part, 2))
            else:
                following.append(
                    scatter_start(links, total, sslots[stage + 1][p], sum_index, chip, core, part, stage + 1)
                )
        flights = following
    swaps = []
    for stage in (2, 1, 0):
        following = []
        for p, part in enumerate(SUM_PARTS):
            for copy in flights[p]:
                copy.wait_recv()
            if stage > 0:
                following.append(gather_start(links, summed, sum_index, chip, core, part, stage - 1))
            else:
                whole = summed.at[sum_index(core, part, {})]
                swaps.append(links.start(whole, whole, sibling))
        flights = following
    spread_out = pltpu.make_async_copy(stack.at[pl.ds(EIG_ROW, Q)], spread_hbm, local_sems.at[4])
    spread_out.start()
    for copy in swaps:
        copy.wait_recv()
    sums_out = pltpu.make_async_copy(summed, sums_hbm, local_sems.at[5])
    sums_out.start()
    links.wait_sends()
    pick_out.wait()
    spread_out.wait()
    sums_out.wait()


def update_kernel(weights_ref, part_ref, eig_ref, scale_ref, pick_ref, spread_ref, out_ref, residual_ref):
    part = part_ref[...]
    reduced = lax.dot_general(part, eig_ref[...], NT, preferred_element_type=F32)
    coefficients = (reduced * scale_ref[...]).astype(BF16)
    step = jnp.dot(coefficients, spread_ref[...], preferred_element_type=F32)
    step -= jnp.dot(part, pick_ref[...], preferred_element_type=F32)
    out_ref[...] = (weights_ref[...].astype(F32) + learn_rate * step).astype(BF16)
    residual_ref[...] = part


def body(centers, weights, labels, loader, sample_ids, nys_ids, eigen_vectors, eigen_scale):
    vmem, anywhere = pl.BlockSpec(memory_space=pltpu.VMEM), pl.BlockSpec(memory_space=pl.ANY)
    weights_t = weights.T
    scratch = [
        pltpu.VMEM((C_DEV, D), BF16),
        pltpu.VMEM((OUT, C_DEV), BF16),
        pltpu.VMEM((OUT, C_DEV), BF16),
        pltpu.VMEM((BATCH, C_DEV), BF16),
        pltpu.VMEM((ROWS, C_DEV), BF16),
        pltpu.VMEM((C_DEV, BATCH), BF16),
        pltpu.VMEM((2, 4, 4, 32, D), BF16),
        pltpu.VMEM((2, 4, 4, 32, D), BF16),
        pltpu.VMEM((HALF, D), BF16),
        pltpu.VMEM((C_DEV, 1), F32),
        pltpu.VMEM((HALF, 128), F32),
        pltpu.VMEM((8, HALF), F32),
        pltpu.VMEM((4, 4, 80, BATCH), BF16),
        pltpu.VMEM((4, 4, 80, BATCH), BF16),
        pltpu.VMEM((40, 512), F32),
        pltpu.VMEM((4, 40, 128), F32),
        pltpu.VMEM((BATCH, 128), F32),
        pltpu.VMEM((4, 4, 32, D), BF16),
        pltpu.VMEM((4, 4, 80, HALF), BF16),
    ]
    for stage in range(3):
        scratch += [pltpu.VMEM((3,) + bcast_shape(part, part[1][: stage + 1]), BF16) for part in BCAST_PARTS]
    for stage in range(3):
        scratch += [pltpu.VMEM((3,) + sum_shape(part, part[1][: stage + 1]), BF16) for part in SUM_PARTS]
    count = 3 + 1 + 36 + 2 + 4 + 54 + 3
    scratch += [pltpu.SemaphoreType.DMA((count,)), pltpu.SemaphoreType.DMA((count,)), pltpu.SemaphoreType.DMA((6,))]
    sums, pick, spread = pl.pallas_call(
        step_kernel,
        out_shape=(
            jax.ShapeDtypeStruct((4, 4, 80, BATCH), BF16),
            jax.ShapeDtypeStruct((BATCH, C_DEV), BF16),
            jax.ShapeDtypeStruct((Q, C_DEV), BF16),
        ),
        in_specs=[pl.BlockSpec(memory_space=pltpu.SMEM), vmem, vmem, vmem, anywhere, anywhere, anywhere],
        out_specs=(anywhere, anywhere, anywhere),
        scratch_shapes=scratch,
        compiler_params=pltpu.CompilerParams(
            collective_id=0, has_side_effects=True, vmem_limit_bytes=58 * 2**20
        ),
        name="step",
    )(loader, sample_ids.reshape(1, BATCH), nys_ids.reshape(1, NYS_DEV), eigen_vectors.T, centers, weights_t, labels.T)
    sums = sums.reshape(ROWS, BATCH)
    new_weights, residual = pl.pallas_call(
        update_kernel,
        grid=(4,),
        out_shape=(jax.ShapeDtypeStruct((OUT, C_DEV), BF16), jax.ShapeDtypeStruct((OUT, BATCH), BF16)),
        in_specs=[
            pl.BlockSpec((256, C_DEV), lambda i: (i, 0)),
            pl.BlockSpec((256, BATCH), lambda i: (i, 0)),
            pl.BlockSpec((Q, BATCH), lambda i: (0, 0)),
            pl.BlockSpec((1, Q), lambda i: (0, 0)),
            pl.BlockSpec((BATCH, C_DEV), lambda i: (0, 0)),
            pl.BlockSpec((Q, C_DEV), lambda i: (0, 0)),
        ],
        out_specs=(
            pl.BlockSpec((256, C_DEV), lambda i: (i, 0)),
            pl.BlockSpec((256, BATCH), lambda i: (i, 0)),
        ),
        compiler_params=pltpu.CompilerParams(vmem_limit_bytes=40 * 2**20),
        name="update",
    )(weights_t, sums, lax.slice_in_dim(sums, EIG_ROW, EIG_ROW + Q, axis=0), eigen_scale.reshape(1, Q), pick, spread)
    return (new_weights.T, residual.T)


def solution(mesh):
    placed = (
        P(("centers", "nys"), None),
        P(("centers", "nys"), None),
        P(("centers", "nys"), None),
        P(),
        P(),
        P(("centers", "nys")),
        P("centers", "nys"),
        P(),
    )
    return jax.shard_map(
        body,
        mesh=mesh,
        in_specs=placed,
        out_specs=(P(("centers", "nys"), None), P()),
        check_vma=False,
    )
```

```python
import jax
import jax.numpy as jnp
from jax import lax
from jax.experimental import pallas as pl
from jax.experimental.pallas import tpu as pltpu
from jax.sharding import PartitionSpec as P

MESH = pl.DeviceIdType.MESH
BF16, F32 = jnp.bfloat16, jnp.float32

learn_rate = 0.5
kernel_width = 0.25

D, OUT, Q, BATCH, C_DEV, NYS_DEV = 1024, 1000, 160, 1024, 2048, 128
QUARTER = BATCH // 4
ROWS = 1280
EIG_ROW = 1008
BCAST_PARTS = (((0, 384), (0, 1, 2)), ((384, 384), (1, 2, 0)), ((768, 256), (2, 0, 1)))
SUM_PARTS = (((0, 32), (0, 1, 2)), ((512, 32), (1, 2, 0)), ((1024, 16), (2, 0, 1)))
NT = (((1,), (1,)), ((), ()))


def position():
    c, n = lax.axis_index("centers"), lax.axis_index("nys")
    x, y = lax.rem(c, 4), lax.div(c, 8)
    z = lax.rem(lax.div(c, 4), 2) * 2 + lax.div(n, 2)
    return (x, y, z), lax.rem(n, 2)


def device(chip, core):
    x, y, z = chip
    return ((y * 2 + lax.div(z, 2)) * 4 + x, lax.rem(z, 2) * 2 + core)


def peer_at(chip, core, axis, step):
    moved = list(chip)
    moved[axis] = lax.rem(chip[axis] + step, 4)
    return moved[axis], device(moved, core)


def span(value, count):
    return pl.ds(pl.multiple_of(value * count, count), count)


def bcast_index(quarter, part, v0, v1=None):
    (first, count), _ = part
    second = pl.ds(0, 4) if v1 is None else pl.ds(v1, 1)
    return (pl.ds(quarter, 1), second, pl.ds(v0, 1), pl.ds(0, 16), pl.ds(first, count))


def sum_index(quarter, part, v0, v1=None):
    (first, count), _ = part
    start, rows = (v0 * 4 * count, 4 * count) if v1 is None else ((v0 * 4 + v1) * count, count)
    return (pl.ds(quarter, 1), pl.ds(pl.multiple_of(first + start, 16), rows), pl.ds(0, QUARTER))


def bcast_shape(part, stage):
    return (1, 4 if stage == 0 else 1, 1, 16, part[0][1])


def sum_shape(part, stage):
    return (1, part[0][1] * (4 if stage == 0 else 1), QUARTER)


class Links:
    def __init__(self, core, send_sems, recv_sems):
        self.core, self.send_sems, self.recv_sems, self.copies = core, send_sems, recv_sems, []

    def start(self, source, target, to):
        i = len(self.copies)
        copy = pltpu.make_async_remote_copy(
            src_ref=source, dst_ref=target, send_sem=self.send_sems.at[i], recv_sem=self.recv_sems.at[i],
            device_id=to, device_id_type=MESH,
        )
        copy.start()
        self.copies.append(copy)
        return copy

    def wait_sends(self):
        for copy in self.copies:
            copy.wait_send()


STEPS = (2, 1, 3)


class Reduction:
    def __init__(self, links, index, parts, buffer, result, slots, chip, quarter):
        self.links, self.index, self.parts, self.buffer, self.result = links, index, parts, buffer, result
        self.slots, self.chip, self.quarter = slots, chip, quarter
        self.flights = [[] for _ in parts]

    def at(self, p, *places):
        return self.index(self.quarter, self.parts[p], *places)

    def own(self, p, count):
        return self.at(p, *(self.chip[a] for a in self.parts[p][1][:count]))

    def peer(self, p, stage, step):
        return peer_at(self.chip, self.links.core, self.parts[p][1][stage], step)

    def scatter_first(self, p, step):
        place, to = self.peer(p, 0, step)
        self.flights[p].append(self.links.start(self.buffer.at[self.at(p, place)], self.slots[0][p].at[step - 1], to))

    def scatter_all(self):
        for p in range(len(self.parts)):
            for step in STEPS:
                self.scatter_first(p, step)

    def arrive(self, p):
        for copy in self.flights[p]:
            copy.wait_recv()

    def add(self, p, stage):
        self.arrive(p)
        own = self.own(p, stage + 1)
        got = self.buffer[own].astype(F32)
        for step in range(3):
            got += self.slots[stage][p][step].astype(F32)
        return own, got.astype(BF16)

    def send(self, p, stage, ref):
        self.flights[p] = [self.links.start(ref, ref, self.peer(p, stage, step)[1]) for step in STEPS]

    def second(self):
        for p in range(len(self.parts)):
            own, got = self.add(p, 0)
            self.buffer[own] = got
            mine, self.flights[p] = self.chip[self.parts[p][1][0]], []
            for step in STEPS:
                place, to = self.peer(p, 1, step)
                self.flights[p].append(
                    self.links.start(self.buffer.at[self.at(p, mine, place)], self.slots[1][p].at[step - 1], to)
                )

    def exchange(self):
        for p in range(len(self.parts)):
            _, got = self.add(p, 1)
            place = self.chip[self.parts[p][1][2]]
            self.slots[2][p][place] = got
            self.send(p, 2, self.slots[2][p].at[place])

    def gather_second(self):
        for p in range(len(self.parts)):
            self.arrive(p)
            got = self.slots[2][p][0].astype(F32)
            for place in range(1, 4):
                got += self.slots[2][p][place].astype(F32)
            own = self.own(p, 2)
            self.result[own] = got.astype(BF16)
            self.send(p, 1, self.result.at[own])

    def gather_first(self):
        for p in range(len(self.parts)):
            self.arrive(p)
            self.send(p, 0, self.result.at[self.own(p, 1)])

    def swap(self, sibling):
        for p in range(len(self.parts)):
            self.arrive(p)
        ref = self.result.at[self.quarter]
        return self.links.start(ref, ref, sibling)


def step_kernel(
    loader_ref, ids_ref, nys_ref, eig_ref, scale_ref, centers_hbm, weights_hbm, labels_hbm,
    new_hbm, res_hbm,
    cent, wts, labs, pick, stack, kern, cand, mini, cnorm, ncol, mnorm, total, summed,
    own_eig, got_eig, idcol, half_c, half_s, steps, partial, *rest,
):
    bslots = [[rest[9 * u + 3 * s : 9 * u + 3 * s + 3] for s in range(3)] for u in range(2)]
    sslots = [[rest[18 + 9 * u + 3 * s : 21 + 9 * u + 3 * s] for s in range(3)] for u in range(2)]
    send_sems, recv_sems, local_sems = rest[36:]
    chip, core = position()
    other = 1 - core
    links = Links(core, send_sems, recv_sems)
    sibling = device(chip, other)
    my_nys = lax.axis_index("nys")
    near = chip[0], chip[1], chip[2] + 1 - 2 * lax.rem(chip[2], 2)
    partners = [sibling, device(near, other)]
    for axis in range(3):
        partners += [peer_at(chip, core, axis, step)[1] for step in (1, 2, 3)]

    barrier = pltpu.get_barrier_semaphore()
    for to in partners:
        pl.semaphore_signal(barrier, inc=1, device_id=to, device_id_type=MESH)
    loads = [
        pltpu.make_async_copy(a, b, local_sems.at[i])
        for i, (a, b) in enumerate(((centers_hbm, cent), (weights_hbm, wts), (labels_hbm, labs)))
    ]
    loads[0].start()

    away = loader_ref[0] - (lax.axis_index("centers") * 4 + my_nys)
    ids = jnp.minimum(ids_ref[...] + away * away * 4096, 4096).astype(F32)
    idcol[...] = jnp.broadcast_to(ids, (128, BATCH)).T
    own_eig[...] = eig_ref[...].astype(F32)

    def pick_block(block):
        rows = span(block, 256)
        column_ids = idcol[rows, :].astype(jnp.int32)

        def put(k, _):
            lane = lax.broadcasted_iota(jnp.int32, (256, 128), 1) + k * 128
            pick[rows, span(k, 128)] = jnp.where(lane == column_ids, 1.0, 0.0).astype(BF16)
            return 0

        lax.fori_loop(0, 16, put, 0, unroll=4)

    def candidates(quarter):
        rows = span(quarter, 256)

        def put(k, _):
            columns = span(k, 256)
            got = jnp.dot(pick[rows, :], cent[:, columns], preferred_element_type=F32)
            cand[pl.ds(quarter, 1), :, :, :, columns] = got.astype(BF16).reshape(1, 4, 4, 16, 256)
            return 0

        lax.fori_loop(0, 4, put, 0)

    batch = [Reduction(links, bcast_index, BCAST_PARTS, cand, mini, bslots[u], chip, u * 2 + core) for u in range(2)]
    sums = [Reduction(links, sum_index, SUM_PARTS, total, summed, sslots[u], chip, u * 2 + core) for u in range(2)]
    eig_copies = []
    pick_block(other)
    for u in range(2):
        mine, theirs = u * 2 + core, u * 2 + other
        if u == 0:
            loads[0].wait()
            loads[1].start()
            loads[2].start()
        candidates(theirs)
        if u == 0:
            pl.semaphore_wait(barrier, len(partners))
        first = links.start(cand.at[theirs], half_c.at[u], sibling)
        if u == 0:
            for to_core, to_chip in ((other, chip), (core, near), (other, near)):
                to = device(to_chip, to_core)
                eig_copies.append(links.start(own_eig.at[:, span(to[1], 128)], got_eig.at[my_nys], to))
            got_eig[my_nys] = own_eig[:, span(my_nys, 128)]
        pick_block(mine)
        candidates(mine)
        if u == 0:
            pick_block(2 + other)
        first.wait_recv()

        def add_half(k, _):
            cand[mine, k] = (cand[mine, k].astype(F32) + half_c[u, k].astype(F32)).astype(BF16)
            return 0

        lax.fori_loop(0, 4, add_half, 0)
        batch[u].scatter_all()
    def targets(x):
        def put(k, _):
            wanted = pick[span(k, 256), :]
            if x < 3:
                got = lax.dot_general(labs[pl.ds(x * 320, 320), :], wanted, NT, preferred_element_type=F32)
            else:
                got = lax.dot_general(labs[pl.ds(960, 40), :], wanted, NT, preferred_element_type=F32)
                got = jnp.concatenate([got, jnp.zeros((280, 256), F32)], axis=0)
            total[k, pl.ds(x * 320, 320), :] = got.astype(BF16)
            return 0

        lax.fori_loop(0, 4, put, 0)

    def center_norms():
        def put(k, _):
            rows = span(k, 64)
            norm = jnp.sum(jnp.square(cent[rows, :].astype(F32)), axis=1, keepdims=True)
            cnorm[rows, :] = jnp.broadcast_to(norm, (64, 128))
            return 0

        lax.fori_loop(0, 32, put, 0)

    def stack_rows():
        loads[1].wait()

        def put(k, _):
            rows = span(k, 64)
            stack[rows, :] = wts[rows, :]
            return 0

        lax.fori_loop(0, 15, put, 0)

    def stack_tail():
        for copy in eig_copies:
            copy.wait_recv()
        vectors = got_eig[...].reshape(Q, NYS_DEV).astype(BF16)
        row_ids = jnp.broadcast_to(nys_ref[...].astype(F32), (128, 128)).T.astype(jnp.int32)

        def put(k, _):
            columns = span(k, 128)
            lane = lax.broadcasted_iota(jnp.int32, (128, 128), 1) + k * 128
            chosen = jnp.where(lane == row_ids, 1.0, 0.0).astype(BF16)
            spread = jnp.dot(vectors, chosen, preferred_element_type=F32)
            tail = jnp.concatenate(
                [wts[pl.ds(960, 40), columns].astype(F32), jnp.zeros((8, 128), F32), spread, jnp.zeros((112, 128), F32)],
                axis=0,
            )
            stack[pl.ds(960, 320), columns] = tail.astype(BF16)
            return 0

        lax.fori_loop(0, 16, put, 0)

    def kernel_quarter(quarter, midway=None):
        def rows_of(k, _):
            block = mini[quarter, k].reshape(64, D)
            norm = jnp.sum(jnp.square(block.astype(F32)), axis=1, keepdims=True)
            ncol[span(k, 64), :] = jnp.broadcast_to(norm, (64, 128))
            return 0

        lax.fori_loop(0, 4, rows_of, 0)
        mnorm[...] = ncol[...].T[0:8, :]

        def inner(k):
            rows = mini[quarter].reshape(256, D)
            return lax.dot_general(cent[pl.ds(k * 256, 256), :], rows, NT, preferred_element_type=F32)

        following = inner(0)
        for k in range(8):
            current = following
            if k < 7:
                following = inner(k + 1)
            if k == 4 and midway is not None:
                midway()
            rows = pl.ds(k * 256, 256)
            for j in range(2):
                lanes = pl.ds(j * 128, 128)
                square = cnorm[rows, :] + mnorm[0:1, lanes] - 2.0 * current[:, j * 128 : (j + 1) * 128]
                square = jnp.minimum(jnp.maximum(square, 1e-30), 3e38)
                distance = square * lax.rsqrt(square)
                kern[quarter, rows, lanes] = jnp.exp(distance * (-1.0 / kernel_width)).astype(BF16)

    def product(quarter, step):
        places = [lax.rem(chip[axes[0]] + step, 4) for _, axes in SUM_PARTS]
        slices = [sum_index(quarter, part, place)[1] for part, place in zip(SUM_PARTS, places)]
        rows = jnp.concatenate([stack[at, :] for at in slices], axis=0)
        got = jnp.dot(rows, kern[quarter], preferred_element_type=F32)
        pieces, start = [], 0
        for part, at in zip(SUM_PARTS, slices):
            count = 4 * part[0][1]
            pieces.append((at, got[start : start + count] - total[quarter, at, :].astype(F32)))
            start += count
        return pieces

    def their_products(u):
        copies = []
        for step in STEPS + (0,):
            copies.append([])
            for at, got in product(u * 2 + other, step):
                ref = total.at[u * 2 + other, at, :]
                ref[...] = got.astype(BF16)
                copies[-1].append(links.start(ref, half_s.at[u, at, :], sibling))
        return copies

    def own_products(u, copies):
        for i, step in enumerate(STEPS + (0,)):
            for p, (at, got) in enumerate(product(u * 2 + core, step)):
                copies[i][p].wait_recv()
                total[u * 2 + core, at, :] = (got + half_s[u, at, :].astype(F32)).astype(BF16)
                if step:
                    sums[u].scatter_first(p, step)

    def residual_of(u):
        return jnp.concatenate([summed[2 * u, pl.ds(0, EIG_ROW), :], summed[2 * u + 1, pl.ds(0, EIG_ROW), :]], axis=1)

    def reduced_of(u):
        eigs = [summed[2 * u + h, pl.ds(EIG_ROW, Q), :] for h in range(2)]
        return lax.dot_general(residual_of(u), jnp.concatenate(eigs, axis=1), NT, preferred_element_type=F32)

    def taken(u, k):
        return jnp.dot(residual_of(u), pick[pl.ds(u * 512, 512), pl.ds(k * 512, 512)], preferred_element_type=F32)

    def residual_out(u):
        outs = []
        for q in (2 * u, 2 * u + 1):
            columns = pl.ds(q * 256, 256)
            labs[:, columns] = summed[q, pl.ds(0, OUT), :]
            outs.append(pltpu.make_async_copy(labs.at[:, columns], res_hbm.at[:, columns], local_sems.at[3 + q]))
            outs[-1].start()
        return outs

    stack_rows()
    stack_tail()
    loads[2].wait()
    targets(0)
    for chunk in batch:
        chunk.second()
    targets(1)
    for chunk in batch:
        chunk.exchange()
    targets(2)
    for chunk in batch:
        chunk.gather_second()
    targets(3)
    for chunk in batch:
        chunk.gather_first()
    center_norms()
    swaps = [batch[0].swap(sibling)]
    kernel_quarter(core)
    swaps[0].wait_recv()
    swaps.append(batch[1].swap(sibling))
    kernel_quarter(other)
    own_products(0, their_products(0))
    kernel_quarter(2 + core)
    swaps[1].wait_recv()
    kernel_quarter(2 + other, sums[0].second)
    copies = their_products(1)
    sums[0].exchange()
    own_products(1, copies)
    sums[0].gather_second()
    sums[1].second()
    sums[0].gather_first()
    sums[1].exchange()
    sums[1].gather_second()
    first = sums[0].swap(sibling)
    first.wait_recv()
    outs = residual_out(0)
    for k in range(2):
        steps[:, pl.ds(k * 512, 512)] = taken(0, k)
    sums[1].gather_first()
    for k in range(2, 4):
        steps[:, pl.ds(k * 512, 512)] = taken(0, k)
    partial[...] = reduced_of(0)
    first = sums[1].swap(sibling)
    first.wait_recv()
    outs += residual_out(1)
    coefficients = ((partial[...] + reduced_of(1)) * scale_ref[...]).astype(BF16)
    for k in range(4):
        columns = pl.ds(k * 512, 512)
        step = jnp.dot(coefficients, stack[pl.ds(EIG_ROW, Q), columns], preferred_element_type=F32)
        step -= steps[:, columns] + taken(1, k)
        wts[:, columns] = (wts[:, columns].astype(F32) + learn_rate * step[:OUT]).astype(BF16)
        out = pltpu.make_async_copy(wts.at[:, columns], new_hbm.at[:, columns], local_sems.at[7 + k])
        out.start()
        outs.append(out)
    links.wait_sends()
    for out in outs:
        out.wait()


def body(centers, weights, labels, loader, sample_ids, nys_ids, eigen_vectors, eigen_scale):
    vmem, anywhere = pl.BlockSpec(memory_space=pltpu.VMEM), pl.BlockSpec(memory_space=pl.ANY)
    scratch = [
        pltpu.VMEM((C_DEV, D), BF16),
        pltpu.VMEM((OUT, C_DEV), BF16),
        pltpu.VMEM((OUT, C_DEV), BF16),
        pltpu.VMEM((BATCH, C_DEV), BF16),
        pltpu.VMEM((ROWS, C_DEV), BF16),
        pltpu.VMEM((4, C_DEV, QUARTER), BF16),
        pltpu.VMEM((4, 4, 4, 16, D), BF16),
        pltpu.VMEM((4, 4, 4, 16, D), BF16),
        pltpu.VMEM((C_DEV, 128), F32),
        pltpu.VMEM((256, 128), F32),
        pltpu.VMEM((8, 256), F32),
        pltpu.VMEM((4, ROWS, QUARTER), BF16),
        pltpu.VMEM((4, ROWS, QUARTER), BF16),
        pltpu.VMEM((40, 512), F32),
        pltpu.VMEM((4, 40, 128), F32),
        pltpu.VMEM((BATCH, 128), F32),
        pltpu.VMEM((2, 4, 4, 16, D), BF16),
        pltpu.VMEM((2, ROWS, QUARTER), BF16),
        pltpu.VMEM((EIG_ROW, C_DEV), F32),
        pltpu.VMEM((EIG_ROW, Q), F32),
    ]
    for parts, shape in ((BCAST_PARTS, bcast_shape), (SUM_PARTS, sum_shape)):
        for stage in (0, 1, 2, 0, 1, 2):
            scratch += [pltpu.VMEM((3 + stage // 2,) + shape(part, stage), BF16) for part in parts]
    count = 3 + 2 * (1 + 45 + 1) + 2 * (12 + 45 + 1)
    scratch += [pltpu.SemaphoreType.DMA((count,)), pltpu.SemaphoreType.DMA((count,)), pltpu.SemaphoreType.DMA((11,))]
    new_weights, residual = pl.pallas_call(
        step_kernel,
        out_shape=(
            jax.ShapeDtypeStruct((OUT, C_DEV), BF16),
            jax.ShapeDtypeStruct((OUT, BATCH), BF16),
        ),
        in_specs=[pl.BlockSpec(memory_space=pltpu.SMEM), vmem, vmem, vmem, vmem, anywhere, anywhere, anywhere],
        out_specs=(anywhere, anywhere),
        scratch_shapes=scratch,
        compiler_params=pltpu.CompilerParams(
            collective_id=0, has_side_effects=True, vmem_limit_bytes=62 * 2**20
        ),
        name="step",
    )(
        loader, sample_ids.reshape(1, BATCH), nys_ids.reshape(1, NYS_DEV), eigen_vectors.T, eigen_scale.reshape(1, Q),
        centers, weights.T, labels.T,
    )
    return (new_weights.T, residual.T)


def solution(mesh):
    placed = (
        P(("centers", "nys"), None),
        P(("centers", "nys"), None),
        P(("centers", "nys"), None),
        P(),
        P(),
        P(("centers", "nys")),
        P("centers", "nys"),
        P(),
    )
    return jax.shard_map(
        body,
        mesh=mesh,
        in_specs=placed,
        out_specs=(P(("centers", "nys"), None), P()),
        check_vma=False,
    )
```

```python
import jax
import jax.numpy as jnp
from jax import lax
from jax.experimental import pallas as pl
from jax.experimental.pallas import tpu as pltpu
from jax.sharding import PartitionSpec as P

MESH = pl.DeviceIdType.MESH
BF16, F32 = jnp.bfloat16, jnp.float32

learn_rate = 0.5
kernel_width = 0.25

D, OUT, Q, BATCH, C_DEV, NYS_DEV = 1024, 1000, 160, 1024, 2048, 128
QUARTER = BATCH // 4
ROWS = 1280
EIG_ROW = 1008
BCAST_PARTS = (((0, 384), (0, 1, 2)), ((384, 384), (1, 2, 0)), ((768, 256), (2, 0, 1)))
SUM_PARTS = (((0, 32), (0, 1, 2)), ((512, 32), (1, 2, 0)), ((1024, 16), (2, 0, 1)))
NT = (((1,), (1,)), ((), ()))


def position():
    c, n = lax.axis_index("centers"), lax.axis_index("nys")
    x, y = lax.rem(c, 4), lax.div(c, 8)
    z = lax.rem(lax.div(c, 4), 2) * 2 + lax.div(n, 2)
    return (x, y, z), lax.rem(n, 2)


def device(chip, core):
    x, y, z = chip
    return ((y * 2 + lax.div(z, 2)) * 4 + x, lax.rem(z, 2) * 2 + core)


def peer_at(chip, core, axis, step):
    moved = list(chip)
    moved[axis] = lax.rem(chip[axis] + step, 4)
    return moved[axis], device(moved, core)


def span(value, count):
    return pl.ds(pl.multiple_of(value * count, count), count)


def bcast_index(quarter, part, v0, v1=None):
    (first, count), _ = part
    second = pl.ds(0, 4) if v1 is None else pl.ds(v1, 1)
    return (pl.ds(quarter, 1), second, pl.ds(v0, 1), pl.ds(0, 16), pl.ds(first, count))


def sum_index(quarter, part, v0, v1=None):
    (first, count), _ = part
    start, rows = (v0 * 4 * count, 4 * count) if v1 is None else ((v0 * 4 + v1) * count, count)
    return (pl.ds(quarter, 1), pl.ds(pl.multiple_of(first + start, 16), rows), pl.ds(0, QUARTER))


def bcast_shape(part, stage):
    return (1, 4 if stage == 0 else 1, 1, 16, part[0][1])


def sum_shape(part, stage):
    return (1, part[0][1] * (4 if stage == 0 else 1), QUARTER)


class Links:
    def __init__(self, core, send_sems, recv_sems):
        self.core, self.send_sems, self.recv_sems, self.copies, self.count = core, send_sems, recv_sems, [], 0

    def start(self, source, target, to):
        i = self.count + len(self.copies)
        copy = pltpu.make_async_remote_copy(
            src_ref=source, dst_ref=target, send_sem=self.send_sems.at[i], recv_sem=self.recv_sems.at[i],
            device_id=to, device_id_type=MESH,
        )
        copy.start()
        self.copies.append(copy)
        return copy

    def wait_sends(self):
        for copy in self.copies:
            copy.wait_send()
        self.copies, self.count = [], self.count + len(self.copies)


STEPS = (2, 1, 3)


class Reduction:
    def __init__(self, links, index, parts, buffer, result, slots, chip, quarter):
        self.links, self.index, self.parts, self.buffer, self.result = links, index, parts, buffer, result
        self.slots, self.chip, self.quarter = slots, chip, quarter
        self.flights = [[] for _ in parts]

    def at(self, p, *places):
        return self.index(self.quarter, self.parts[p], *places)

    def own(self, p, count):
        return self.at(p, *(self.chip[a] for a in self.parts[p][1][:count]))

    def peer(self, p, stage, step):
        return peer_at(self.chip, self.links.core, self.parts[p][1][stage], step)

    def scatter_first(self, p, step):
        place, to = self.peer(p, 0, step)
        self.flights[p].append(self.links.start(self.buffer.at[self.at(p, place)], self.slots[0][p].at[step - 1], to))

    def scatter_all(self):
        for p in range(len(self.parts)):
            for step in STEPS:
                self.scatter_first(p, step)

    def arrive(self, p):
        for copy in self.flights[p]:
            copy.wait_recv()

    def add(self, p, stage):
        self.arrive(p)
        own = self.own(p, stage + 1)
        got = self.buffer[own].astype(F32)
        for step in range(3):
            got += self.slots[stage][p][step].astype(F32)
        return own, got.astype(BF16)

    def send(self, p, stage, ref):
        self.flights[p] = [self.links.start(ref, ref, self.peer(p, stage, step)[1]) for step in STEPS]

    def second(self):
        for p in range(len(self.parts)):
            own, got = self.add(p, 0)
            self.buffer[own] = got
            mine, self.flights[p] = self.chip[self.parts[p][1][0]], []
            for step in STEPS:
                place, to = self.peer(p, 1, step)
                self.flights[p].append(
                    self.links.start(self.buffer.at[self.at(p, mine, place)], self.slots[1][p].at[step - 1], to)
                )

    def exchange(self):
        for p in range(len(self.parts)):
            _, got = self.add(p, 1)
            place = self.chip[self.parts[p][1][2]]
            self.slots[2][p][place] = got
            self.send(p, 2, self.slots[2][p].at[place])

    def gather_second(self):
        for p in range(len(self.parts)):
            self.arrive(p)
            got = self.slots[2][p][0].astype(F32)
            for place in range(1, 4):
                got += self.slots[2][p][place].astype(F32)
            own = self.own(p, 2)
            self.result[own] = got.astype(BF16)
            self.send(p, 1, self.result.at[own])

    def gather_first(self):
        for p in range(len(self.parts)):
            self.arrive(p)
            self.send(p, 0, self.result.at[self.own(p, 1)])

    def swap(self, sibling):
        for p in range(len(self.parts)):
            self.arrive(p)
        ref = self.result.at[self.quarter]
        return self.links.start(ref, ref, sibling)


def step_kernel(
    loader_ref, ids_ref, nys_ref, eig_ref, scale_ref, centers_hbm, weights_hbm, labels_hbm,
    base_hbm, res_hbm, coef_hbm, late_hbm, spread_hbm,
    cent, wts, labs, pick, stack, kern, cand, mini, cnorm, turned, mnorm, total, summed,
    own_eig, got_eig, idcol, half_c, half_s, partial, coef, *rest,
):
    bslots = [[rest[9 * u + 3 * s : 9 * u + 3 * s + 3] for s in range(3)] for u in range(2)]
    sslots = [[rest[18 + 9 * u + 3 * s : 21 + 9 * u + 3 * s] for s in range(3)] for u in range(2)]
    send_sems, recv_sems, local_sems = rest[36:]
    chip, core = position()
    other = 1 - core
    links = Links(core, send_sems, recv_sems)
    sibling = device(chip, other)
    my_nys = lax.axis_index("nys")
    near = chip[0], chip[1], chip[2] + 1 - 2 * lax.rem(chip[2], 2)
    partners = [sibling, device(near, other)]
    for axis in range(3):
        partners += [peer_at(chip, core, axis, step)[1] for step in (1, 2, 3)]

    barrier = pltpu.get_barrier_semaphore()
    for to in partners:
        pl.semaphore_signal(barrier, inc=1, device_id=to, device_id_type=MESH)
    loads = [
        pltpu.make_async_copy(a, b, local_sems.at[i])
        for i, (a, b) in enumerate(((centers_hbm, cent), (weights_hbm, wts), (labels_hbm, labs)))
    ]
    loads[0].start()

    away = loader_ref[0] - (lax.axis_index("centers") * 4 + my_nys)
    ids = jnp.minimum(ids_ref[...] + away * away * 4096, 4096).astype(F32)
    idcol[...] = jnp.broadcast_to(ids, (128, BATCH)).T
    own_eig[...] = eig_ref[...].astype(F32)

    def pick_block(block):
        rows = span(block, 256)
        column_ids = idcol[rows, :].astype(jnp.int32)

        def put(k, _):
            lane = lax.broadcasted_iota(jnp.int32, (256, 128), 1) + k * 128
            pick[rows, span(k, 128)] = jnp.where(lane == column_ids, 1.0, 0.0).astype(BF16)
            return 0

        lax.fori_loop(0, 16, put, 0, unroll=4)

    def candidates(quarter):
        rows = span(quarter, 256)

        def put(k, _):
            columns = span(k, 256)
            got = jnp.dot(pick[rows, :], cent[:, columns], preferred_element_type=F32)
            cand[pl.ds(quarter, 1), :, :, :, columns] = got.astype(BF16).reshape(1, 4, 4, 16, 256)
            return 0

        lax.fori_loop(0, 4, put, 0)

    batch = [Reduction(links, bcast_index, BCAST_PARTS, cand, mini, bslots[u], chip, u * 2 + core) for u in range(2)]
    sums = [Reduction(links, sum_index, SUM_PARTS, total, summed, sslots[u], chip, u * 2 + core) for u in range(2)]
    eig_copies = []
    for block in (other, core, 2 + other):
        pick_block(block)
    for u in range(2):
        mine, theirs = u * 2 + core, u * 2 + other
        if u == 0:
            loads[0].wait()
            loads[1].start()
            loads[2].start()
        candidates(theirs)
        if u == 0:
            pl.semaphore_wait(barrier, len(partners))
        first = links.start(cand.at[theirs], half_c.at[u], sibling)
        if u == 0:
            for to_core, to_chip in ((other, chip), (core, near), (other, near)):
                to = device(to_chip, to_core)
                eig_copies.append(links.start(own_eig.at[:, span(to[1], 128)], got_eig.at[my_nys], to))
            got_eig[my_nys] = own_eig[:, span(my_nys, 128)]
        if u == 1:
            pick_block(mine)
        candidates(mine)
        first.wait_recv()

        def add_half(k, _):
            cand[mine, k] = (cand[mine, k].astype(F32) + half_c[u, k].astype(F32)).astype(BF16)
            return 0

        lax.fori_loop(0, 4, add_half, 0)
        batch[u].scatter_all()
    def targets(quarter):
        wanted = pick[pl.ds(quarter * 256, 256), :]
        got = lax.dot_general(labs[...], wanted, NT, preferred_element_type=F32)
        got = jnp.concatenate([got, jnp.zeros((ROWS - OUT, 256), F32)], axis=0)
        total[quarter] = got.astype(BF16)

    def center_norms():
        def put(k, _):
            rows = span(k, 64)
            norm = jnp.sum(jnp.square(cent[rows, :].astype(F32)), axis=1, keepdims=True)
            cnorm[rows, :] = jnp.broadcast_to(norm, (64, 128))
            return 0

        lax.fori_loop(0, 32, put, 0)

    def stack_rows():
        loads[1].wait()

        def put(k, _):
            rows = span(k, 64)
            stack[rows, :] = wts[rows, :]
            return 0

        lax.fori_loop(0, 15, put, 0)

    def stack_tail():
        for copy in eig_copies:
            copy.wait_recv()
        vectors = got_eig[...].reshape(Q, NYS_DEV).astype(BF16)
        row_ids = jnp.broadcast_to(nys_ref[...].astype(F32), (128, 128)).T.astype(jnp.int32)

        def put(k, _):
            columns = span(k, 128)
            lane = lax.broadcasted_iota(jnp.int32, (128, 128), 1) + k * 128
            chosen = jnp.where(lane == row_ids, 1.0, 0.0).astype(BF16)
            spread = jnp.dot(vectors, chosen, preferred_element_type=F32)
            tail = jnp.concatenate(
                [wts[pl.ds(960, 40), columns].astype(F32), jnp.zeros((8, 128), F32), spread, jnp.zeros((112, 128), F32)],
                axis=0,
            )
            stack[pl.ds(960, 320), columns] = tail.astype(BF16)
            return 0

        lax.fori_loop(0, 16, put, 0)

    def kernel_quarter(quarter, midway=None):
        turned[...] = mini[quarter].reshape(256, D).T
        mnorm[...] = jnp.broadcast_to(jnp.sum(jnp.square(turned[...].astype(F32)), axis=0, keepdims=True), (8, 256))

        def inner(k):
            return jnp.dot(cent[pl.ds(k * 256, 256), :], turned[...], preferred_element_type=F32)

        following = inner(0)
        for k in range(8):
            current = following
            if k < 7:
                following = inner(k + 1)
            if k == 4 and midway is not None:
                midway()
            rows = pl.ds(k * 256, 256)
            for j in range(2):
                lanes = pl.ds(j * 128, 128)
                square = cnorm[rows, :] + mnorm[0:1, lanes] - 2.0 * current[:, j * 128 : (j + 1) * 128]
                square = jnp.minimum(jnp.maximum(square, 1e-30), 3e38)
                distance = square * lax.rsqrt(square)
                kern[quarter, rows, lanes] = jnp.exp(distance * (-1.0 / kernel_width)).astype(BF16)

    def product(quarter, step):
        places = [lax.rem(chip[axes[0]] + step, 4) for _, axes in SUM_PARTS]
        slices = [sum_index(quarter, part, place)[1] for part, place in zip(SUM_PARTS, places)]
        rows = jnp.concatenate([stack[at, :] for at in slices], axis=0)
        got = jnp.dot(rows, kern[quarter], preferred_element_type=F32)
        pieces, start = [], 0
        for part, at in zip(SUM_PARTS, slices):
            count = 4 * part[0][1]
            pieces.append((at, got[start : start + count] - total[quarter, at, :].astype(F32)))
            start += count
        return pieces

    def their_products(u):
        copies = []
        for step in STEPS + (0,):
            copies.append([])
            for at, got in product(u * 2 + other, step):
                ref = total.at[u * 2 + other, at, :]
                ref[...] = got.astype(BF16)
                copies[-1].append(links.start(ref, half_s.at[u, at, :], sibling))
        return copies

    def own_products(u, copies):
        for i, step in enumerate(STEPS + (0,)):
            for p, (at, got) in enumerate(product(u * 2 + core, step)):
                copies[i][p].wait_recv()
                total[u * 2 + core, at, :] = (got + half_s[u, at, :].astype(F32)).astype(BF16)
                if step:
                    sums[u].scatter_first(p, step)

    def residual_of(u):
        return jnp.concatenate([summed[2 * u, pl.ds(0, EIG_ROW), :], summed[2 * u + 1, pl.ds(0, EIG_ROW), :]], axis=1)

    def reduced_of(u):
        eigs = [summed[2 * u + h, pl.ds(EIG_ROW, Q), :] for h in range(2)]
        return lax.dot_general(residual_of(u), jnp.concatenate(eigs, axis=1), NT, preferred_element_type=F32)

    def base_block(k):
        columns = pl.ds(k * 512, 512)
        taken = jnp.dot(residual_of(0), pick[pl.ds(0, 512), columns], preferred_element_type=F32)
        wts[:, columns] = (wts[:, columns].astype(F32) - learn_rate * taken[:OUT]).astype(BF16)
        out = pltpu.make_async_copy(wts.at[:, columns], base_hbm.at[:, columns], local_sems.at[7 + k])
        out.start()
        return out

    def residual_out(u):
        outs = []
        for q in (2 * u, 2 * u + 1):
            columns = pl.ds(q * 256, 256)
            labs[:, columns] = summed[q, pl.ds(0, OUT), :]
            outs.append(pltpu.make_async_copy(labs.at[:, columns], res_hbm.at[:, columns], local_sems.at[3 + q]))
            outs[-1].start()
        return outs

    stack_rows()
    stack_tail()
    early = [
        pltpu.make_async_copy(idcol.at[pl.ds(512, 512), :], late_hbm, local_sems.at[12]),
        pltpu.make_async_copy(stack.at[pl.ds(EIG_ROW, Q), :], spread_hbm, local_sems.at[13]),
    ]
    loads[2].wait()
    for out in early:
        out.start()
    targets(0)
    for chunk in batch:
        chunk.second()
    targets(1)
    for chunk in batch:
        chunk.exchange()
    targets(2)
    for chunk in batch:
        chunk.gather_second()
    targets(3)
    for chunk in batch:
        chunk.gather_first()
    center_norms()
    swaps = [batch[0].swap(sibling)]
    kernel_quarter(core)
    swaps[0].wait_recv()
    swaps.append(batch[1].swap(sibling))
    kernel_quarter(other)
    own_products(0, their_products(0))
    kernel_quarter(2 + core)
    swaps[1].wait_recv()
    kernel_quarter(2 + other, sums[0].second)
    copies = their_products(1)
    sums[0].exchange()
    own_products(1, copies)
    sums[0].gather_second()
    sums[1].second()
    sums[0].gather_first()
    sums[1].exchange()
    sums[1].gather_second()
    first = sums[0].swap(sibling)
    first.wait_recv()
    outs = residual_out(0) + early
    outs += [base_block(k) for k in range(2)]
    sums[1].gather_first()
    outs += [base_block(k) for k in range(2, 4)]
    partial[...] = reduced_of(0)
    links.wait_sends()
    first = sums[1].swap(sibling)
    first.wait_recv()
    outs += residual_out(1)
    coef[...] = ((partial[...] + reduced_of(1)) * scale_ref[...])[:OUT].astype(BF16)
    outs.append(pltpu.make_async_copy(coef, coef_hbm, local_sems.at[11]))
    outs[-1].start()
    links.wait_sends()
    for out in outs:
        out.wait()


def finish_kernel(base_ref, late_ref, part_ref, coef_ref, ids_ref, spread_ref, new_ref, res_ref):
    ids = ids_ref[...].astype(jnp.int32) - pl.program_id(0) * 512
    lane = lax.broadcasted_iota(jnp.int32, (512, 128), 1)
    pick = jnp.concatenate([jnp.where(lane + j * 128 == ids, 1.0, 0.0).astype(BF16) for j in range(4)], axis=1)
    step = jnp.dot(coef_ref[...], spread_ref[...], preferred_element_type=F32)
    step -= jnp.dot(late_ref[...], pick, preferred_element_type=F32)
    new_ref[...] = (base_ref[...].astype(F32) + learn_rate * step).astype(BF16)
    res_ref[...] = part_ref[...]


def body(centers, weights, labels, loader, sample_ids, nys_ids, eigen_vectors, eigen_scale):
    vmem, anywhere = pl.BlockSpec(memory_space=pltpu.VMEM), pl.BlockSpec(memory_space=pl.ANY)
    scratch = [
        pltpu.VMEM((C_DEV, D), BF16),
        pltpu.VMEM((OUT, C_DEV), BF16),
        pltpu.VMEM((OUT, C_DEV), BF16),
        pltpu.VMEM((BATCH, C_DEV), BF16),
        pltpu.VMEM((ROWS, C_DEV), BF16),
        pltpu.VMEM((4, C_DEV, QUARTER), BF16),
        pltpu.VMEM((4, 4, 4, 16, D), BF16),
        pltpu.VMEM((4, 4, 4, 16, D), BF16),
        pltpu.VMEM((C_DEV, 128), F32),
        pltpu.VMEM((D, QUARTER), BF16),
        pltpu.VMEM((8, 256), F32),
        pltpu.VMEM((4, ROWS, QUARTER), BF16),
        pltpu.VMEM((4, ROWS, QUARTER), BF16),
        pltpu.VMEM((40, 512), F32),
        pltpu.VMEM((4, 40, 128), F32),
        pltpu.VMEM((BATCH, 128), F32),
        pltpu.VMEM((2, 4, 4, 16, D), BF16),
        pltpu.VMEM((2, ROWS, QUARTER), BF16),
        pltpu.VMEM((EIG_ROW, Q), F32),
        pltpu.VMEM((OUT, Q), BF16),
    ]
    for parts, shape in ((BCAST_PARTS, bcast_shape), (SUM_PARTS, sum_shape)):
        for stage in (0, 1, 2, 0, 1, 2):
            scratch += [pltpu.VMEM((3 + stage // 2,) + shape(part, stage), BF16) for part in parts]
    count = 3 + 2 * (1 + 45 + 1) + 2 * (12 + 45 + 1)
    scratch += [pltpu.SemaphoreType.DMA((count,)), pltpu.SemaphoreType.DMA((count,)), pltpu.SemaphoreType.DMA((14,))]
    base, residual, coef, late_ids, spread = pl.pallas_call(
        step_kernel,
        out_shape=(
            jax.ShapeDtypeStruct((OUT, C_DEV), BF16),
            jax.ShapeDtypeStruct((OUT, BATCH), BF16),
            jax.ShapeDtypeStruct((OUT, Q), BF16),
            jax.ShapeDtypeStruct((512, 128), F32),
            jax.ShapeDtypeStruct((Q, C_DEV), BF16),
        ),
        in_specs=[pl.BlockSpec(memory_space=pltpu.SMEM), vmem, vmem, vmem, vmem, anywhere, anywhere, anywhere],
        out_specs=(anywhere,) * 5,
        scratch_shapes=scratch,
        compiler_params=pltpu.CompilerParams(
            collective_id=0, has_side_effects=True, vmem_limit_bytes=62 * 2**20
        ),
        name="step",
    )(
        loader, sample_ids.reshape(1, BATCH), nys_ids.reshape(1, NYS_DEV), eigen_vectors.T, eigen_scale.reshape(1, Q),
        centers, weights.T, labels.T,
    )
    new_weights, residual = pl.pallas_call(
        finish_kernel,
        out_shape=(
            jax.ShapeDtypeStruct((OUT, C_DEV), BF16),
            jax.ShapeDtypeStruct((OUT, BATCH), BF16),
        ),
        grid=(4,),
        in_specs=[
            pl.BlockSpec((OUT, 512), lambda i: (0, i)),
            pl.BlockSpec((OUT, 512), lambda i: (0, 1)),
            pl.BlockSpec((OUT, 256), lambda i: (0, i)),
            pl.BlockSpec((OUT, Q), lambda i: (0, 0)),
            pl.BlockSpec((512, 128), lambda i: (0, 0)),
            pl.BlockSpec((Q, 512), lambda i: (0, i)),
        ],
        out_specs=(pl.BlockSpec((OUT, 512), lambda i: (0, i)), pl.BlockSpec((OUT, 256), lambda i: (0, i))),
        compiler_params=pltpu.CompilerParams(vmem_limit_bytes=60 * 2**20),
        name="finish",
    )(base, residual, residual, coef, late_ids, spread)
    return (new_weights.T, residual.T)


def solution(mesh):
    placed = (
        P(("centers", "nys"), None),
        P(("centers", "nys"), None),
        P(("centers", "nys"), None),
        P(),
        P(),
        P(("centers", "nys")),
        P("centers", "nys"),
        P(),
    )
    return jax.shard_map(
        body,
        mesh=mesh,
        in_specs=placed,
        out_specs=(P(("centers", "nys"), None), P()),
        check_vma=False,
    )
```

```python
import jax
import jax.numpy as jnp
from jax import lax
from jax.experimental import pallas as pl
from jax.experimental.pallas import tpu as pltpu
from jax.sharding import PartitionSpec as P

MESH = pl.DeviceIdType.MESH
BF16, F32 = jnp.bfloat16, jnp.float32

learn_rate = 0.5
kernel_width = 0.25

D, OUT, Q, BATCH, C_DEV, NYS_DEV = 1024, 1000, 160, 1024, 2048, 128
QUARTER = BATCH // 4
ROWS = 1280
EIG_ROW = 1008
BCAST_PARTS = (((0, 384), (0, 1, 2)), ((384, 384), (1, 2, 0)), ((768, 256), (2, 0, 1)))
SUM_PARTS = (((0, 32), (0, 1, 2)), ((512, 32), (1, 2, 0)), ((1024, 16), (2, 0, 1)))
NT = (((1,), (1,)), ((), ()))


def position():
    c, n = lax.axis_index("centers"), lax.axis_index("nys")
    x, y = lax.rem(c, 4), lax.div(c, 8)
    z = lax.rem(lax.div(c, 4), 2) * 2 + lax.div(n, 2)
    return (x, y, z), lax.rem(n, 2)


def device(chip, core):
    x, y, z = chip
    return ((y * 2 + lax.div(z, 2)) * 4 + x, lax.rem(z, 2) * 2 + core)


def peer_at(chip, core, axis, step):
    moved = list(chip)
    moved[axis] = lax.rem(chip[axis] + step, 4)
    return moved[axis], device(moved, core)


def span(value, count):
    return pl.ds(pl.multiple_of(value * count, count), count)


def bcast_index(quarter, part, v0, v1=None):
    (first, count), _ = part
    second = pl.ds(0, 4) if v1 is None else pl.ds(v1, 1)
    return (pl.ds(quarter, 1), second, pl.ds(v0, 1), pl.ds(0, 16), pl.ds(first, count))


def sum_index(quarter, part, v0, v1=None):
    (first, count), _ = part
    start, rows = (v0 * 4 * count, 4 * count) if v1 is None else ((v0 * 4 + v1) * count, count)
    return (pl.ds(quarter, 1), pl.ds(pl.multiple_of(first + start, 16), rows), pl.ds(0, QUARTER))


def bcast_shape(part, stage):
    return (1, 4 if stage == 0 else 1, 1, 16, part[0][1])


def sum_shape(part, stage):
    return (1, part[0][1] * (4 if stage == 0 else 1), QUARTER)


class Links:
    def __init__(self, core, send_sems, recv_sems):
        self.core, self.send_sems, self.recv_sems, self.copies, self.count = core, send_sems, recv_sems, [], 0

    def start(self, source, target, to):
        i = self.count + len(self.copies)
        copy = pltpu.make_async_remote_copy(
            src_ref=source, dst_ref=target, send_sem=self.send_sems.at[i], recv_sem=self.recv_sems.at[i],
            device_id=to, device_id_type=MESH,
        )
        copy.start()
        self.copies.append(copy)
        return copy

    def wait_sends(self):
        for copy in self.copies:
            copy.wait_send()
        self.copies, self.count = [], self.count + len(self.copies)


STEPS = (2, 1, 3)


class Reduction:
    def __init__(self, links, index, parts, buffer, result, slots, chip, quarter):
        self.links, self.index, self.parts, self.buffer, self.result = links, index, parts, buffer, result
        self.slots, self.chip, self.quarter = slots, chip, quarter
        self.flights = [[] for _ in parts]

    def at(self, p, *places):
        return self.index(self.quarter, self.parts[p], *places)

    def own(self, p, count):
        return self.at(p, *(self.chip[a] for a in self.parts[p][1][:count]))

    def peer(self, p, stage, step):
        return peer_at(self.chip, self.links.core, self.parts[p][1][stage], step)

    def scatter_first(self, p, step):
        place, to = self.peer(p, 0, step)
        self.flights[p].append(self.links.start(self.buffer.at[self.at(p, place)], self.slots[0][p].at[step - 1], to))

    def scatter_all(self):
        for p in range(len(self.parts)):
            for step in STEPS:
                self.scatter_first(p, step)

    def arrive(self, p):
        for copy in self.flights[p]:
            copy.wait_recv()

    def add(self, p, stage):
        self.arrive(p)
        own = self.own(p, stage + 1)
        got = self.buffer[own].astype(F32)
        for step in range(3):
            got += self.slots[stage][p][step].astype(F32)
        return own, got.astype(BF16)

    def send(self, p, stage, ref):
        self.flights[p] = [self.links.start(ref, ref, self.peer(p, stage, step)[1]) for step in STEPS]

    def second(self):
        for p in range(len(self.parts)):
            own, got = self.add(p, 0)
            self.buffer[own] = got
            mine, self.flights[p] = self.chip[self.parts[p][1][0]], []
            for step in STEPS:
                place, to = self.peer(p, 1, step)
                self.flights[p].append(
                    self.links.start(self.buffer.at[self.at(p, mine, place)], self.slots[1][p].at[step - 1], to)
                )

    def exchange(self):
        for p in range(len(self.parts)):
            _, got = self.add(p, 1)
            place = self.chip[self.parts[p][1][2]]
            self.slots[2][p][place] = got
            self.send(p, 2, self.slots[2][p].at[place])

    def gather_second(self):
        for p in range(len(self.parts)):
            self.arrive(p)
            got = self.slots[2][p][0].astype(F32)
            for place in range(1, 4):
                got += self.slots[2][p][place].astype(F32)
            own = self.own(p, 2)
            self.result[own] = got.astype(BF16)
            self.send(p, 1, self.result.at[own])

    def gather_first(self):
        for p in range(len(self.parts)):
            self.arrive(p)
            self.send(p, 0, self.result.at[self.own(p, 1)])

    def swap(self, sibling):
        for p in range(len(self.parts)):
            self.arrive(p)
        ref = self.result.at[self.quarter]
        return self.links.start(ref, ref, sibling)


def step_kernel(
    loader_ref, ids_ref, nys_ref, eig_ref, scale_ref, centers_hbm, weights_hbm, labels_hbm,
    base_hbm, res_hbm, coef_hbm, late_hbm, spread_hbm,
    cent, wts, labs, pick, stack, kern, cand, mini, cnorm, turned, mnorm, total, summed,
    own_eig, got_eig, idcol, half_c, half_s, partial, coef, *rest,
):
    bslots = [[rest[9 * u + 3 * s : 9 * u + 3 * s + 3] for s in range(3)] for u in range(2)]
    sslots = [[rest[18 + 9 * u + 3 * s : 21 + 9 * u + 3 * s] for s in range(3)] for u in range(2)]
    send_sems, recv_sems, local_sems = rest[36:]
    chip, core = position()
    other = 1 - core
    links = Links(core, send_sems, recv_sems)
    sibling = device(chip, other)
    my_nys = lax.axis_index("nys")
    near = chip[0], chip[1], chip[2] + 1 - 2 * lax.rem(chip[2], 2)
    partners = [sibling, device(near, other)]
    for axis in range(3):
        partners += [peer_at(chip, core, axis, step)[1] for step in (1, 2, 3)]

    barrier = pltpu.get_barrier_semaphore()
    for to in partners:
        pl.semaphore_signal(barrier, inc=1, device_id=to, device_id_type=MESH)
    loads = [
        pltpu.make_async_copy(a, b, local_sems.at[i])
        for i, (a, b) in enumerate(((centers_hbm, cent), (weights_hbm, wts), (labels_hbm, labs)))
    ]
    loads[0].start()

    away = loader_ref[0] - (lax.axis_index("centers") * 4 + my_nys)
    ids = jnp.minimum(ids_ref[...] + away * away * 4096, 4096).astype(F32)
    idcol[...] = jnp.broadcast_to(ids, (128, BATCH)).T
    own_eig[...] = eig_ref[...].astype(F32)

    def pick_block(block):
        rows = span(block, 256)
        column_ids = idcol[rows, :].astype(jnp.int32)

        def put(k, _):
            lane = lax.broadcasted_iota(jnp.int32, (256, 128), 1) + k * 128
            pick[rows, span(k, 128)] = jnp.where(lane == column_ids, 1.0, 0.0).astype(BF16)
            return 0

        lax.fori_loop(0, 16, put, 0, unroll=4)

    def candidates(quarter):
        rows = span(quarter, 256)

        def put(k, _):
            columns = span(k, 256)
            got = jnp.dot(pick[rows, :], cent[:, columns], preferred_element_type=F32)
            cand[pl.ds(quarter, 1), :, :, :, columns] = got.astype(BF16).reshape(1, 4, 4, 16, 256)
            return 0

        lax.fori_loop(0, 4, put, 0)

    batch = [Reduction(links, bcast_index, BCAST_PARTS, cand, mini, bslots[u], chip, u * 2 + core) for u in range(2)]
    sums = [Reduction(links, sum_index, SUM_PARTS, total, summed, sslots[u], chip, u * 2 + core) for u in range(2)]
    eig_copies = []
    for block in (other, core, 2 + other):
        pick_block(block)
    for u in range(2):
        mine, theirs = u * 2 + core, u * 2 + other
        if u == 0:
            loads[0].wait()
            loads[1].start()
            loads[2].start()
        candidates(theirs)
        if u == 0:
            pl.semaphore_wait(barrier, len(partners))
        first = links.start(cand.at[theirs], half_c.at[u], sibling)
        if u == 0:
            for to_core, to_chip in ((other, chip), (core, near), (other, near)):
                to = device(to_chip, to_core)
                eig_copies.append(links.start(own_eig.at[:, span(to[1], 128)], got_eig.at[my_nys], to))
            got_eig[my_nys] = own_eig[:, span(my_nys, 128)]
        if u == 1:
            pick_block(mine)
        candidates(mine)
        first.wait_recv()

        def add_half(k, _):
            cand[mine, k] = (cand[mine, k].astype(F32) + half_c[u, k].astype(F32)).astype(BF16)
            return 0

        lax.fori_loop(0, 4, add_half, 0)
        batch[u].scatter_all()
    def targets(quarter):
        wanted = pick[pl.ds(quarter * 256, 256), :]
        got = lax.dot_general(labs[...], wanted, NT, preferred_element_type=F32)
        got = jnp.concatenate([got, jnp.zeros((ROWS - OUT, 256), F32)], axis=0)
        total[quarter] = got.astype(BF16)

    def center_norms():
        def put(k, _):
            rows = span(k, 64)
            norm = jnp.sum(jnp.square(cent[rows, :].astype(F32)), axis=1, keepdims=True)
            cnorm[rows, :] = jnp.broadcast_to(norm, (64, 128))
            return 0

        lax.fori_loop(0, 32, put, 0)

    def stack_rows():
        loads[1].wait()

        def put(k, _):
            rows = span(k, 64)
            stack[rows, :] = wts[rows, :]
            return 0

        lax.fori_loop(0, 15, put, 0)

    def stack_tail():
        for copy in eig_copies:
            copy.wait_recv()
        vectors = got_eig[...].reshape(Q, NYS_DEV).astype(BF16)
        row_ids = jnp.broadcast_to(nys_ref[...].astype(F32), (128, 128)).T.astype(jnp.int32)

        def put(k, _):
            columns = span(k, 128)
            lane = lax.broadcasted_iota(jnp.int32, (128, 128), 1) + k * 128
            chosen = jnp.where(lane == row_ids, 1.0, 0.0).astype(BF16)
            spread = jnp.dot(vectors, chosen, preferred_element_type=F32)
            tail = jnp.concatenate(
                [wts[pl.ds(960, 40), columns].astype(F32), jnp.zeros((8, 128), F32), spread, jnp.zeros((112, 128), F32)],
                axis=0,
            )
            stack[pl.ds(960, 320), columns] = tail.astype(BF16)
            return 0

        lax.fori_loop(0, 16, put, 0)

    def kernel_quarter(quarter, midway=None):
        turned[...] = mini[quarter].reshape(256, D).T
        mnorm[...] = jnp.broadcast_to(jnp.sum(jnp.square(turned[...].astype(F32)), axis=0, keepdims=True), (8, 256))

        def inner(k):
            return jnp.dot(cent[pl.ds(k * 256, 256), :], turned[...], preferred_element_type=F32)

        following = inner(0)
        for k in range(8):
            current = following
            if k < 7:
                following = inner(k + 1)
            if k == 4 and midway is not None:
                midway()
            rows = pl.ds(k * 256, 256)
            for j in range(2):
                lanes = pl.ds(j * 128, 128)
                square = cnorm[rows, :] + mnorm[0:1, lanes] - 2.0 * current[:, j * 128 : (j + 1) * 128]
                square = jnp.minimum(jnp.maximum(square, 1e-30), 3e38)
                distance = square * lax.rsqrt(square)
                kern[quarter, rows, lanes] = jnp.exp(distance * (-1.0 / kernel_width)).astype(BF16)

    def product(quarter, step):
        places = [lax.rem(chip[axes[0]] + step, 4) for _, axes in SUM_PARTS]
        slices = [sum_index(quarter, part, place)[1] for part, place in zip(SUM_PARTS, places)]
        rows = jnp.concatenate([stack[at, :] for at in slices], axis=0)
        got = jnp.dot(rows, kern[quarter], preferred_element_type=F32)
        pieces, start = [], 0
        for part, at in zip(SUM_PARTS, slices):
            count = 4 * part[0][1]
            pieces.append((at, got[start : start + count] - total[quarter, at, :].astype(F32)))
            start += count
        return pieces

    def their_products(u):
        copies = []
        for step in STEPS + (0,):
            copies.append([])
            for at, got in product(u * 2 + other, step):
                ref = total.at[u * 2 + other, at, :]
                ref[...] = got.astype(BF16)
                copies[-1].append(links.start(ref, half_s.at[u, at, :], sibling))
        return copies

    def own_products(u, copies):
        for i, step in enumerate(STEPS + (0,)):
            for p, (at, got) in enumerate(product(u * 2 + core, step)):
                copies[i][p].wait_recv()
                total[u * 2 + core, at, :] = (got + half_s[u, at, :].astype(F32)).astype(BF16)
                if step:
                    sums[u].scatter_first(p, step)

    def residual_of(u):
        return jnp.concatenate([summed[2 * u, pl.ds(0, EIG_ROW), :], summed[2 * u + 1, pl.ds(0, EIG_ROW), :]], axis=1)

    def reduced_of(u):
        eigs = [summed[2 * u + h, pl.ds(EIG_ROW, Q), :] for h in range(2)]
        return lax.dot_general(residual_of(u), jnp.concatenate(eigs, axis=1), NT, preferred_element_type=F32)

    def base_block(k):
        columns = pl.ds(k * 512, 512)
        taken = jnp.dot(residual_of(0), pick[pl.ds(0, 512), columns], preferred_element_type=F32)
        wts[:, columns] = (wts[:, columns].astype(F32) - learn_rate * taken[:OUT]).astype(BF16)
        out = pltpu.make_async_copy(wts.at[:, columns], base_hbm.at[:, columns], local_sems.at[7 + k])
        out.start()
        return out

    def residual_out(u):
        outs = []
        for q in (2 * u, 2 * u + 1):
            columns = pl.ds(q * 256, 256)
            labs[:, columns] = summed[q, pl.ds(0, OUT), :]
            outs.append(pltpu.make_async_copy(labs.at[:, columns], res_hbm.at[:, columns], local_sems.at[3 + q]))
            outs[-1].start()
        return outs

    loads[2].wait()
    targets(0)
    targets(1)
    for chunk in batch:
        chunk.second()
    targets(2)
    for chunk in batch:
        chunk.exchange()
    targets(3)
    for chunk in batch:
        chunk.gather_second()
    center_norms()
    for chunk in batch:
        chunk.gather_first()
    stack_rows()
    stack_tail()
    early = [
        pltpu.make_async_copy(idcol.at[pl.ds(512, 512), :], late_hbm, local_sems.at[12]),
        pltpu.make_async_copy(stack.at[pl.ds(EIG_ROW, Q), :], spread_hbm, local_sems.at[13]),
    ]
    for out in early:
        out.start()
    swaps = [batch[0].swap(sibling)]
    kernel_quarter(core)
    swaps[0].wait_recv()
    swaps.append(batch[1].swap(sibling))
    kernel_quarter(other)
    own_products(0, their_products(0))
    kernel_quarter(2 + core)
    swaps[1].wait_recv()
    kernel_quarter(2 + other, sums[0].second)
    copies = their_products(1)
    sums[0].exchange()
    own_products(1, copies)
    sums[0].gather_second()
    sums[1].second()
    sums[1].exchange()
    sums[0].gather_first()
    sums[1].gather_second()
    first = sums[0].swap(sibling)
    first.wait_recv()
    outs = residual_out(0) + early
    outs += [base_block(k) for k in range(2)]
    sums[1].gather_first()
    outs += [base_block(k) for k in range(2, 4)]
    partial[...] = reduced_of(0)
    links.wait_sends()
    first = sums[1].swap(sibling)
    first.wait_recv()
    outs += residual_out(1)
    coef[...] = ((partial[...] + reduced_of(1)) * scale_ref[...])[:OUT].astype(BF16)
    outs.append(pltpu.make_async_copy(coef, coef_hbm, local_sems.at[11]))
    outs[-1].start()
    links.wait_sends()
    for out in outs:
        out.wait()


def finish_kernel(base_ref, late_ref, part_ref, coef_ref, ids_ref, spread_ref, new_ref, res_ref):
    ids = ids_ref[...].astype(jnp.int32) - pl.program_id(0) * 512
    lane = lax.broadcasted_iota(jnp.int32, (512, 128), 1)
    pick = jnp.concatenate([jnp.where(lane + j * 128 == ids, 1.0, 0.0).astype(BF16) for j in range(4)], axis=1)
    step = jnp.dot(coef_ref[...], spread_ref[...], preferred_element_type=F32)
    step -= jnp.dot(late_ref[...], pick, preferred_element_type=F32)
    new_ref[...] = (base_ref[...].astype(F32) + learn_rate * step).astype(BF16)
    res_ref[...] = part_ref[...]


def body(centers, weights, labels, loader, sample_ids, nys_ids, eigen_vectors, eigen_scale):
    vmem, anywhere = pl.BlockSpec(memory_space=pltpu.VMEM), pl.BlockSpec(memory_space=pl.ANY)
    scratch = [
        pltpu.VMEM((C_DEV, D), BF16),
        pltpu.VMEM((OUT, C_DEV), BF16),
        pltpu.VMEM((OUT, C_DEV), BF16),
        pltpu.VMEM((BATCH, C_DEV), BF16),
        pltpu.VMEM((ROWS, C_DEV), BF16),
        pltpu.VMEM((4, C_DEV, QUARTER), BF16),
        pltpu.VMEM((4, 4, 4, 16, D), BF16),
        pltpu.VMEM((4, 4, 4, 16, D), BF16),
        pltpu.VMEM((C_DEV, 128), F32),
        pltpu.VMEM((D, QUARTER), BF16),
        pltpu.VMEM((8, 256), F32),
        pltpu.VMEM((4, ROWS, QUARTER), BF16),
        pltpu.VMEM((4, ROWS, QUARTER), BF16),
        pltpu.VMEM((40, 512), F32),
        pltpu.VMEM((4, 40, 128), F32),
        pltpu.VMEM((BATCH, 128), F32),
        pltpu.VMEM((2, 4, 4, 16, D), BF16),
        pltpu.VMEM((2, ROWS, QUARTER), BF16),
        pltpu.VMEM((EIG_ROW, Q), F32),
        pltpu.VMEM((OUT, Q), BF16),
    ]
    for parts, shape in ((BCAST_PARTS, bcast_shape), (SUM_PARTS, sum_shape)):
        for stage in (0, 1, 2, 0, 1, 2):
            scratch += [pltpu.VMEM((3 + stage // 2,) + shape(part, stage), BF16) for part in parts]
    count = 3 + 2 * (1 + 45 + 1) + 2 * (12 + 45 + 1)
    scratch += [pltpu.SemaphoreType.DMA((count,)), pltpu.SemaphoreType.DMA((count,)), pltpu.SemaphoreType.DMA((14,))]
    base, residual, coef, late_ids, spread = pl.pallas_call(
        step_kernel,
        out_shape=(
            jax.ShapeDtypeStruct((OUT, C_DEV), BF16),
            jax.ShapeDtypeStruct((OUT, BATCH), BF16),
            jax.ShapeDtypeStruct((OUT, Q), BF16),
            jax.ShapeDtypeStruct((512, 128), F32),
            jax.ShapeDtypeStruct((Q, C_DEV), BF16),
        ),
        in_specs=[pl.BlockSpec(memory_space=pltpu.SMEM), vmem, vmem, vmem, vmem, anywhere, anywhere, anywhere],
        out_specs=(anywhere,) * 5,
        scratch_shapes=scratch,
        compiler_params=pltpu.CompilerParams(
            collective_id=0, has_side_effects=True, vmem_limit_bytes=62 * 2**20
        ),
        name="step",
    )(
        loader, sample_ids.reshape(1, BATCH), nys_ids.reshape(1, NYS_DEV), eigen_vectors.T, eigen_scale.reshape(1, Q),
        centers, weights.T, labels.T,
    )
    new_weights, residual = pl.pallas_call(
        finish_kernel,
        out_shape=(
            jax.ShapeDtypeStruct((OUT, C_DEV), BF16),
            jax.ShapeDtypeStruct((OUT, BATCH), BF16),
        ),
        grid=(4,),
        in_specs=[
            pl.BlockSpec((OUT, 512), lambda i: (0, i)),
            pl.BlockSpec((OUT, 512), lambda i: (0, 1)),
            pl.BlockSpec((OUT, 256), lambda i: (0, i)),
            pl.BlockSpec((OUT, Q), lambda i: (0, 0)),
            pl.BlockSpec((512, 128), lambda i: (0, 0)),
            pl.BlockSpec((Q, 512), lambda i: (0, i)),
        ],
        out_specs=(pl.BlockSpec((OUT, 512), lambda i: (0, i)), pl.BlockSpec((OUT, 256), lambda i: (0, i))),
        compiler_params=pltpu.CompilerParams(vmem_limit_bytes=60 * 2**20),
        name="finish",
    )(base, residual, residual, coef, late_ids, spread)
    return (new_weights.T, residual.T)


def solution(mesh):
    placed = (
        P(("centers", "nys"), None),
        P(("centers", "nys"), None),
        P(("centers", "nys"), None),
        P(),
        P(),
        P(("centers", "nys")),
        P("centers", "nys"),
        P(),
    )
    return jax.shard_map(
        body,
        mesh=mesh,
        in_specs=placed,
        out_specs=(P(("centers", "nys"), None), P()),
        check_vma=False,
    )
```
